32 devices in a mesh: inst: 8 (over z, core), tm: 4 (over y, x).
Axes of the slice: x: 2, y: 2, z: 4, core: 2. Of those that a mesh axis runs over, the one named last changes fastest.
Arguments:
- log_prices: bfloat16 [1536, 8192], P('tm', 'inst'), may hold values from -40 to 40
- scaling_filter: float32 [16], replicated, may hold values from -1.5 to 1.5
Outputs:
- variation: float32 [8192, 2, 8192], P('tm', None, 'inst')
The draws below stay inside these ranges and needn't reach their ends.
All inputs are finite; a program needn't handle non-finite values.
Results may differ from the reference program's by a relative error of at most 0.0003.
Values may be sent and summed in bfloat16 or wider, within the bound.
A program may use at most 192 MiB of HBM per device.

```python
import math
import jax
import jax.numpy as jnp
from jax import lax

INSTR = 8192
TAPS = 16
LEVELS = 2
TICK_DEV = 384
TICKS = 1536
N_TM = 4


def draw_log_prices(key, part):
    key = jax.random.fold_in(key, 11)
    key_inst, key_tick, key_rough = jax.random.split(key, 3)
    inst_scale = jnp.exp(jax.random.uniform(key_inst, (1, INSTR), jnp.float32, math.log(0.4), math.log(4.0)))
    tick_scale = jnp.exp(jax.random.uniform(key_tick, (TICKS, 1), jnp.float32, math.log(0.5), math.log(2.0)))
    base_draw = jnp.clip(jax.random.normal(key_rough, (TICKS, INSTR), jnp.float32), -5.0, 5.0)
    return (base_draw * tick_scale * inst_scale).astype(jnp.bfloat16)


def scatter_about(rng, shape, scale, limit, dtype=jnp.bfloat16):
    array = scale * jax.random.normal(rng, shape, jnp.float32)
    return jnp.clip(array, min=-limit, max=limit).astype(dtype)


def setup_inputs(seed: int = 0) -> dict:
    seeds = jax.random.split(jax.random.key(seed), 3)
    log_prices = draw_log_prices(jax.random.fold_in(seeds[2], 71), 0)
    scaling_filter = scatter_about(seeds[1], (TAPS,), TAPS ** -0.5, 1.5, jnp.float32)
    return dict(log_prices=log_prices, scaling_filter=scaling_filter)


def apply_taps(series, filter_taps, dilation):
    running = filter_taps[0] * series
    for lag_index in range(1, TAPS):
        running = running + filter_taps[lag_index] * jnp.roll(series, lag_index * dilation, axis=0)
    return running


def reference(log_prices, scaling_filter):
    alternating = jnp.where(jnp.arange(TAPS) % 2 == 0, 1.0, -1.0).astype(jnp.float32)
    high_pass = scaling_filter[::-1] * alternating
    smooth = log_prices.astype(jnp.float32)
    details = []
    for level in range(LEVELS):
        dilation = 2 ** level
        details.append(apply_taps(smooth, high_pass, dilation).astype(jnp.bfloat16))
        if level + 1 < LEVELS:
            smooth = apply_taps(smooth, scaling_filter, dilation)
    coefficients = jnp.stack(details)
    energy = jnp.sum(jnp.square(coefficients.astype(jnp.float32)), axis=1)

    def level_gram(level_coef):
        def add_slab(running, slab_index):
            first_row = (slab_index * TICK_DEV).astype(jnp.int32)
            slab_rows = lax.dynamic_slice_in_dim(level_coef, first_row, TICK_DEV, 0)
            product = jnp.dot(slab_rows.T, slab_rows, preferred_element_type=jnp.float32)
            return running + product, None

        start_gram = jnp.zeros((INSTR, INSTR), jnp.float32)
        result, unused = lax.scan(add_slab, start_gram, jnp.arange(N_TM).astype(jnp.int32))
        return result

    grams = lax.map(level_gram, coefficients)
    spread = (energy[:, :, None] + energy[:, None, :] - 2.0 * grams) / TICKS
    return jnp.transpose(spread, (1, 0, 2))
```

```python
import functools

import jax
import jax.numpy as jnp
from jax import lax
from jax.experimental import pallas as pl
from jax.experimental.pallas import tpu as pltpu
from jax.sharding import PartitionSpec as P

TAPS = 16
LEVELS = 2
LAGS = (TAPS - 1) * (2**LEVELS - 1) + 1
HALO = 64
MESH = pl.DeviceIdType.MESH


def chunk_list(slab_rows):
    step = slab_rows // 4
    return [(r, step) for r in range(0, slab_rows, step)]


def gather_kernel(
    tm_size, group_count, chunks,
    x_ref, a_ref, b_ref, z_ref,
    z_send, z_recv, a_send, a_recv, b_send, b_recv, p_send, p_recv, local_sem,
):
    t = lax.axis_index("tm")
    inst = lax.axis_index("inst")
    g = inst // 2
    c = inst % 2
    count = len(chunks)

    barrier = pltpu.get_barrier_semaphore()

    def greet(t2, inst2):
        pl.semaphore_signal(barrier, inc=1, device_id={"tm": t2, "inst": inst2}, device_id_type=MESH)

    pl.when(g > 0)(lambda: greet(t, inst - 2))
    pl.when(g < group_count - 1)(lambda: greet(t, inst + 2))
    greet(t, g * 2 + 1 - c)
    for d in range(1, tm_size):
        greet((t + d) % tm_size, inst)
    expected = tm_size + (g > 0).astype(jnp.int32) + (g < group_count - 1).astype(jnp.int32)
    pl.semaphore_wait(barrier, expected)

    def rows(q):
        return pl.ds(chunks[q][0], chunks[q][1])

    def remote(src, dst, send, recv, t2, inst2):
        return pltpu.make_async_remote_copy(
            src_ref=src, dst_ref=dst, send_sem=send, recv_sem=recv,
            device_id={"tm": t2, "inst": inst2}, device_id_type=MESH,
        )

    def z_copy(k, q, way):
        slab = g - k * way
        src = x_ref if k == 0 else z_ref.at[slab]
        ok = (slab >= 0) & (slab < group_count) & (g + way >= 0) & (g + way < group_count)
        return ok, lambda: remote(
            src.at[rows(q)], z_ref.at[slab, rows(q)],
            z_send.at[(way + 1) // 2, k, q], z_recv.at[slab, q], t, inst + 2 * way,
        )

    def z_arrived(slab, q):
        remote(
            z_ref.at[slab, rows(q)], z_ref.at[slab, rows(q)],
            z_send.at[0, 0, q], z_recv.at[slab, q], t, g * 2 + 1 - c,
        ).wait_recv()

    def a_copy(slab, q):
        return remote(
            z_ref.at[slab, rows(q)], a_ref.at[t, c, rows(q)],
            a_send.at[slab, q], a_recv.at[t, q], slab, inst,
        )

    def a_arrived(s, q):
        remote(
            a_ref.at[s, c, rows(q)], a_ref.at[s, c, rows(q)],
            a_send.at[0, q], a_recv.at[s, q], s, inst,
        ).wait_recv()

    def b_copy(d, q):
        t2 = (t + d) % tm_size
        return remote(
            x_ref.at[rows(q)], b_ref.at[t, rows(q)], b_send.at[d, q], b_recv.at[t, q], t2, inst
        )

    def b_arrived(s, q):
        remote(
            b_ref.at[s, rows(q)], b_ref.at[s, rows(q)], b_send.at[0, q], b_recv.at[s, q], s, inst
        ).wait_recv()

    def p_copy(src, s, q):
        return remote(
            src.at[rows(q)], a_ref.at[s, c, rows(q)],
            p_send.at[s, q], p_recv.at[s, q], t, g * 2 + 1 - c,
        )

    def keep(src, s, q):
        return pltpu.make_async_copy(src.at[rows(q)], a_ref.at[s, c, rows(q)], local_sem.at[s, q])

    own = pltpu.make_async_copy(x_ref, b_ref.at[t], local_sem.at[tm_size, 0])
    own.start()

    def start_if(ok, make):
        pl.when(ok)(lambda: make().start())

    for q in range(count):
        for way in (1, -1):
            start_if(*z_copy(0, q, way))
    own.wait()

    def foreign(slab, q):
        def act():
            z_arrived(slab, q)

        return act

    def handle(k, q):
        for way in (1, -1):
            slab = g - k * way
            have = (slab >= 0) & (slab < group_count)

            @pl.when(have)
            def _():
                z_arrived(slab, q)
                start_if(*z_copy(k, q, way))

                @pl.when(slab != t)
                def _():
                    a_copy(slab, q).start()

                @pl.when(slab == t)
                def _():
                    keep(z_ref.at[slab], t, q).start()
                    p_copy(z_ref.at[slab], t, q).start()

    def settle(q):
        for d in range(1, tm_size):
            s = (t + d) % tm_size
            b_arrived(s, q)

            @pl.when(g == t)
            def _():
                keep(b_ref.at[s], s, q).start()
                p_copy(b_ref.at[s], s, q).start()

            @pl.when(g != t)
            def _():
                a_arrived(s, q)
                p_copy(a_ref.at[s, c], s, q).start()

    for q in range(count):
        for d in range(1, tm_size):
            b_copy(d, q).start()

        @pl.when(g == t)
        def _():
            keep(b_ref.at[t], t, q).start()
            p_copy(b_ref.at[t], t, q).start()

        for k in range(1, group_count):
            handle(k, q)
        if q > 0:
            settle(q - 1)
    settle(count - 1)

    for q in range(count):
        for s in range(tm_size):
            remote(
                a_ref.at[s, 1 - c, rows(q)], a_ref.at[s, 1 - c, rows(q)],
                p_send.at[s, q], p_recv.at[s, q], t, g * 2 + 1 - c,
            ).wait_recv()
            p_copy(x_ref, s, q).wait_send()
            pl.when((g == t) | (s == t))(lambda: keep(x_ref, s, q).wait())
        for k in range(group_count):
            for way in (1, -1):
                ok, make = z_copy(k, q, way)
                pl.when(ok)(lambda: make().wait_send())
        for slab in range(group_count):
            pl.when((slab != g) & (slab != t))(lambda: a_copy(slab, q).wait_send())
        for d in range(1, tm_size):
            b_copy(d, q).wait_send()


def gather(log_prices, tm_size, inst_size):
    slab_rows, cols = log_prices.shape
    group_count = inst_size // 2
    chunks = chunk_list(slab_rows)
    n = len(chunks)
    dma = pltpu.SemaphoreType.DMA
    vmem = pl.BlockSpec(memory_space=pltpu.VMEM)
    return pl.pallas_call(
        functools.partial(gather_kernel, tm_size, group_count, chunks),
        out_shape=[
            jax.ShapeDtypeStruct((tm_size, 2, slab_rows, cols), jnp.bfloat16),
            jax.ShapeDtypeStruct((tm_size, slab_rows, cols), jnp.bfloat16),
        ],
        in_specs=[vmem],
        out_specs=[vmem, vmem],
        scratch_shapes=[
            pltpu.VMEM((group_count, slab_rows, cols), jnp.bfloat16),
            dma((2, group_count, n)), dma((group_count, n)),
            dma((group_count, n)), dma((tm_size, n)),
            dma((tm_size, n)), dma((tm_size, n)),
            dma((tm_size, n)), dma((tm_size, n)),
            dma((tm_size + 1, n)),
        ],
        compiler_params=pltpu.CompilerParams(
            collective_id=0, has_side_effects=True, vmem_limit_bytes=40 * 2**20
        ),
        name="gather_series",
    )(log_prices)


def build_bands(f_ref, band_ref):
    half = band_ref.shape[0] // 4
    low = [f_ref[l] for l in range(TAPS)]
    high = [(-1.0) ** l * low[TAPS - 1 - l] for l in range(TAPS)]
    joint = [None] * LAGS
    for b in range(TAPS):
        for l in range(TAPS):
            term = low[l] * high[b]
            lag = l + 2 * b
            joint[lag] = term if joint[lag] is None else joint[lag] + term
    shape = (half, HALO + half)
    lag = HALO + lax.broadcasted_iota(jnp.int32, shape, 0) - lax.broadcasted_iota(jnp.int32, shape, 1)
    for level, taps in enumerate((high, joint)):
        band = jnp.zeros(shape, jnp.float32)
        for l, weight in enumerate(taps):
            band = jnp.where(lag == l, weight, band)
        head = band.astype(jnp.bfloat16)
        rest = (band - head.astype(jnp.float32)).astype(jnp.bfloat16)
        band_ref[pl.ds(level * half, half), :] = head
        band_ref[pl.ds((2 + level) * half, half), :] = rest


def coefficients(band_ref, window):
    half = band_ref.shape[0] // 4
    both = jnp.dot(band_ref[...], window, preferred_element_type=jnp.float32)
    total = (both[: 2 * half] + both[2 * half :]).astype(jnp.bfloat16)
    return total[:half], total[half:]


def gram_kernel(tm_size, f_ref, a_ref, b_ref, o_ref, band_ref, ca_ref, cb_ref, eb_ref):
    slab_rows = b_ref.shape[1]
    half = slab_rows // 2
    width = a_ref.shape[3]
    cols = b_ref.shape[2]
    ticks = tm_size * slab_rows

    def sweep(load, c_ref, where):
        def slab(s, sums):
            before = (s + tm_size - 1) % tm_size
            sums = list(sums)
            windows = (
                jnp.concatenate(
                    [load(before, slab_rows - HALO, HALO), load(s, 0, half)], 0
                ),
                load(s, half - HALO, HALO + half),
            )
            for h, window in enumerate(windows):
                first = pl.multiple_of(s * slab_rows + h * half, half)
                for level, part in enumerate(coefficients(band_ref, window)):
                    c_ref[level, pl.ds(first, half), where] = part
                    wide = part.astype(jnp.float32)
                    sums[level] = sums[level] + jnp.sum(wide * wide, axis=0, keepdims=True)
            return tuple(sums)

        zero = jnp.zeros((1, width), jnp.float32)
        return lax.fori_loop(0, tm_size, slab, (zero, zero))

    @pl.when(pl.program_id(0) == 0)
    def _():
        build_bands(f_ref, band_ref)
        for n in range(cols // width):
            where = pl.ds(n * width, width)
            sums = sweep(lambda s, r, m: b_ref[s, pl.ds(r, m), where], cb_ref, where)
            for level in range(LEVELS):
                eb_ref[pl.ds(level, 1), where] = sums[level]

    sums = sweep(lambda s, r, m: a_ref[s, 0, pl.ds(r, m), :], ca_ref, pl.ds(0, width))
    for level in range(LEVELS):
        gram = lax.dot_general(
            ca_ref[level], cb_ref[level], (((0,), (0,)), ((), ())),
            preferred_element_type=jnp.float32,
        )
        column = jnp.transpose(jnp.broadcast_to(sums[level], (8, width)))[:, :1]
        row = eb_ref[pl.ds(level, 1), :]
        o_ref[:, level, :] = (column + row - 2.0 * gram) * (1.0 / ticks)


def variation(scaling_filter, a, b):
    tm_size, _, slab_rows, cols = a.shape
    ticks = tm_size * slab_rows
    width = 256
    per_half = cols // width
    half = slab_rows // 2
    return pl.pallas_call(
        functools.partial(gram_kernel, tm_size),
        grid=(2 * per_half,),
        out_shape=jax.ShapeDtypeStruct((2 * cols, LEVELS, cols), jnp.float32),
        in_specs=[
            pl.BlockSpec(memory_space=pltpu.SMEM),
            pl.BlockSpec((tm_size, 1, slab_rows, width), lambda n: (0, n // per_half, 0, n % per_half)),
            pl.BlockSpec((tm_size, slab_rows, cols), lambda n: (0, 0, 0)),
        ],
        out_specs=pl.BlockSpec((width, LEVELS, cols), lambda n: (n, 0, 0)),
        scratch_shapes=[
            pltpu.VMEM((4 * half, HALO + half), jnp.bfloat16),
            pltpu.VMEM((LEVELS, ticks, width), jnp.bfloat16),
            pltpu.VMEM((LEVELS, ticks, cols), jnp.bfloat16),
            pltpu.VMEM((8, cols), jnp.float32),
        ],
        compiler_params=pltpu.CompilerParams(vmem_limit_bytes=48 * 2**20),
        name="variation_tiles",
    )(scaling_filter, a, b)


def solution(mesh):
    tm_size, inst_size = mesh.shape["tm"], mesh.shape["inst"]

    def per_device(log_prices, scaling_filter):
        a, b = gather(log_prices, tm_size, inst_size)
        return variation(scaling_filter, a, b)

    placed = (P("tm", "inst"), P())
    return jax.shard_map(
        per_device, mesh=mesh, in_specs=placed, out_specs=P("tm", None, "inst"), check_vma=False
    )
```
